32 devices in a mesh: chan: 4 (over x, core), tm: 8 (over z, y).
Axes of the slice: x: 2, y: 2, z: 4, core: 2. Of those that a mesh axis runs over, the one named last changes fastest.
Arguments:
- voltages: bfloat16 [64, 8192, 2, 512], P('tm', 'chan'), may hold values from -8 to 8
- window_stations: int32 [2], replicated, may hold values from 0 to 255
- channel_flags: int32 [8192], replicated, may hold values 0 or 1
Outputs:
- rm_spectrum: float32 [8, 32, 2, 2, 1024], P('tm', 'chan')
- leakage: float32 [2, 256], replicated
The draws below stay inside these ranges and needn't reach their ends.
All inputs are finite; a program needn't handle non-finite values.
Results may differ from the reference program's by a relative error of at most 0.012.
Values may be sent and summed in bfloat16 or wider, within the bound.
A program may use at most 192 MiB of HBM per device.

```python
import math
import jax
import jax.numpy as jnp
from jax import lax

STATIONS = 256
CHANNELS = 8192
DEPTH = 1024
WINDOW = 2
TIME_DEV = 8
ITERATIONS = 3
TIME = 64
N_TM = 8


def draw_voltages(key, part):
    first, second, third = jax.random.split(key, 3)
    shape = (TIME, CHANNELS, 2, STATIONS)
    signal = jax.random.normal(first, shape, jnp.float32)
    noise = jax.random.normal(second, shape, jnp.float32)
    gain = jnp.exp(jax.random.uniform(third, (1, CHANNELS, 1, STATIONS), jnp.float32, -0.5, 0.5))
    first_feed = signal * gain
    second_feed = (0.6 * signal + 0.8 * noise) * gain
    both = jnp.stack([first_feed, second_feed], -1).reshape(TIME, CHANNELS, 2, 2 * STATIONS)
    return jnp.clip(both, -8.0, 8.0).astype(jnp.bfloat16)


def touch_ends(result, own_key, least, top_value):
    place = [jax.random.randint(jax.random.fold_in(own_key, axis), (), 0, length) for axis, length in enumerate(result.shape)]
    longest = result.shape.index(max(result.shape))
    next_to = place[:longest] + [(place[longest] + 1) % result.shape[longest]] + place[longest + 1:]
    return result.at[tuple(place)].set(least).at[tuple(next_to)].set(top_value)


def setup_inputs(seed: int = 0) -> dict:
    streams_of = jax.random.split(jax.random.key(seed), 4)
    voltages = draw_voltages(jax.random.fold_in(streams_of[3], 71), 0)
    window_stations = jax.random.randint(streams_of[1], (WINDOW,), 0, STATIONS).astype(jnp.int32)
    channel_flags = touch_ends((jax.random.randint(streams_of[2], (CHANNELS,), 0, 8) < 7).astype(jnp.int32), jax.random.fold_in(streams_of[2], 1), 0, 1)
    return {"voltages": voltages, "window_stations": window_stations, "channel_flags": channel_flags}


def phase_table(first_channel, channel_count):
    chan_pos = (first_channel + jnp.arange(channel_count)).astype(jnp.float32)
    frequency = 1.0 + (chan_pos + 0.5) / CHANNELS
    lambda_sq = 1.0 / (frequency * frequency)
    depth_grid = (jnp.arange(DEPTH).astype(jnp.float32) - DEPTH // 2) * 2.0
    angles = 2.0 * depth_grid[None, :] * (lambda_sq[:, None] - 0.5)
    return (jnp.cos(angles).astype(jnp.bfloat16), jnp.sin(angles).astype(jnp.bfloat16))

def station_terms(leak_real, leak_imag, fields, station_map, window_map):
    far_real = lax.optimization_barrier(jnp.sum(station_map * leak_real[None, :], 1))[:, None]
    far_imag = lax.optimization_barrier(jnp.sum(station_map * leak_imag[None, :], 1))[:, None]
    near_real = lax.optimization_barrier(jnp.sum(window_map * leak_real[None, :], 1))[None, :]
    near_imag = lax.optimization_barrier(jnp.sum(window_map * leak_imag[None, :], 1))[None, :]
    row_real = fields[0] - (far_real * fields[2] + far_imag * fields[3])
    row_imag = fields[1] - (far_real * fields[3] - far_imag * fields[2])
    col_real = fields[4] - (near_real * fields[2] + near_imag * fields[3])
    col_imag = -(fields[5] - (near_imag * fields[2] - near_real * fields[3]))
    numer_real = lax.optimization_barrier(jnp.sum(window_map * lax.optimization_barrier(jnp.sum(row_real, 0))[:, None], 0)) + lax.optimization_barrier(jnp.sum(station_map * lax.optimization_barrier(jnp.sum(col_real, 1))[:, None], 0))
    numer_imag = lax.optimization_barrier(jnp.sum(window_map * lax.optimization_barrier(jnp.sum(row_imag, 0))[:, None], 0)) + lax.optimization_barrier(jnp.sum(station_map * lax.optimization_barrier(jnp.sum(col_imag, 1))[:, None], 0))
    weight_sum = lax.optimization_barrier(jnp.sum(window_map * lax.optimization_barrier(jnp.sum(fields[6], 0))[:, None], 0)) + lax.optimization_barrier(jnp.sum(station_map * lax.optimization_barrier(jnp.sum(fields[7], 1))[:, None], 0))
    return (numer_real, numer_imag, weight_sum)

def reference(voltages, window_stations, channel_flags):
    feed_index = (2 * window_stations[:, None] + jnp.arange(2, dtype=jnp.int32)[None, :]).reshape(-1).astype(jnp.int32)

    def add_shard(shard, total):
        block = lax.dynamic_slice_in_dim(voltages, shard * TIME_DEV, TIME_DEV, 0).astype(jnp.float32)
        picked = jnp.take(block, feed_index, axis=3)
        blocks = jnp.einsum('tcaw,tcbx->cbawx', picked, block, precision=lax.Precision.HIGHEST)
        real_part = blocks[:, 0, 0] + blocks[:, 1, 1]
        imag_part = blocks[:, 0, 1] - blocks[:, 1, 0]
        rounded = lax.optimization_barrier(jnp.stack([real_part, imag_part], 1).astype(jnp.bfloat16))
        return total + rounded.astype(jnp.float32)
    total = lax.fori_loop(0, N_TM, add_shard, jnp.zeros((CHANNELS, 2, 2 * WINDOW, 2 * STATIONS), jnp.float32))
    stored = lax.optimization_barrier(total.astype(jnp.bfloat16))
    six = stored.astype(jnp.float32).reshape(CHANNELS, 2, WINDOW, 2, STATIONS, 2)

    def correlation(feed_a, feed_b):
        return jnp.transpose(six[:, :, :, feed_a, :, feed_b], (1, 3, 2, 0))
    corr_xx = correlation(0, 0)
    corr_xy = correlation(0, 1)
    corr_yx = correlation(1, 0)
    corr_yy = correlation(1, 1)
    flag_weights = channel_flags.astype(jnp.float32)
    pol_real = 0.5 * (corr_xx[0] - corr_yy[0]) - 0.5 * (corr_xy[1] + corr_yx[1])
    pol_imag = 0.5 * (corr_xx[1] - corr_yy[1]) + 0.5 * (corr_xy[0] + corr_yx[0])
    pol_real = (pol_real * flag_weights).astype(jnp.bfloat16).reshape(STATIONS * WINDOW, CHANNELS)
    pol_imag = (pol_imag * flag_weights).astype(jnp.bfloat16).reshape(STATIONS * WINDOW, CHANNELS)
    cosine, sine_part = phase_table(0, CHANNELS)
    out_real = jnp.dot(pol_real, cosine, preferred_element_type=jnp.float32) + jnp.dot(pol_imag, sine_part, preferred_element_type=jnp.float32)
    out_imag = jnp.dot(pol_imag, cosine, preferred_element_type=jnp.float32) - jnp.dot(pol_real, sine_part, preferred_element_type=jnp.float32)
    norm_factor = 1.0 / math.sqrt(CHANNELS * TIME)
    spectrum = jnp.stack([out_real, out_imag], 1) * norm_factor
    rm_spectrum = spectrum.reshape(N_TM, STATIONS // N_TM, WINDOW, 2, DEPTH)

    def conj_sum(left, right):
        real_part = lax.optimization_barrier(jnp.sum(flag_weights * (left[0] * right[0] + left[1] * right[1]), -1)) / CHANNELS
        imag_part = lax.optimization_barrier(jnp.sum(flag_weights * (left[1] * right[0] - left[0] * right[1]), -1)) / CHANNELS
        return (real_part, imag_part)
    cross_real, cross_imag = conj_sum(corr_xy, corr_yy)
    mixed_real, mixed_imag = conj_sum(corr_xx, corr_yy)
    side_real, side_imag = conj_sum(corr_xy, corr_xx)
    power_y = lax.optimization_barrier(jnp.sum(flag_weights * (corr_yy[0] * corr_yy[0] + corr_yy[1] * corr_yy[1]), -1)) / CHANNELS
    power_x = lax.optimization_barrier(jnp.sum(flag_weights * (corr_xx[0] * corr_xx[0] + corr_xx[1] * corr_xx[1]), -1)) / CHANNELS
    fields = [cross_real, cross_imag, mixed_real, mixed_imag, side_real, side_imag, power_y, power_x]
    station_axis = jnp.arange(STATIONS, dtype=jnp.int32)
    window_map = (window_stations[:, None] == station_axis[None, :]).astype(jnp.float32)
    station_map = jnp.eye(STATIONS, dtype=jnp.float32)
    leak_real = jnp.zeros((STATIONS,), jnp.float32)
    leak_imag = jnp.zeros((STATIONS,), jnp.float32)
    for iteration in range(ITERATIONS):
        numer_real, numer_imag, weight_sum = station_terms(leak_real, leak_imag, fields, station_map, window_map)
        leak_real = numer_real / (weight_sum + 1e-06)
        leak_imag = numer_imag / (weight_sum + 1e-06)
    return (rm_spectrum, jnp.stack([leak_real, leak_imag], 0))
```

```python
import math

import jax
import jax.numpy as jnp
from jax import lax
from jax.experimental import pallas as pl
from jax.experimental.pallas import tpu as pltpu
from jax.sharding import PartitionSpec as P

CHANNELS = 8192
DEPTH = 1024
ITERATIONS = 3
GROUP = 16
LANES = 128
NUM_Z = 4
CORES = 2
CHUNKS = 4
F32 = jnp.float32
BF16 = jnp.bfloat16


def correlate_kernel(scalars, x_ref, vis_ref, pol_ref):
    times, _, parts, inputs = x_ref.shape
    depth = times * GROUP * parts
    columns = 8 * GROUP
    row = lax.broadcasted_iota(jnp.int32, (depth, columns), 0)
    col = lax.broadcasted_iota(jnp.int32, (depth, columns), 1)
    same_channel = lax.rem(lax.div(row, parts), GROUP) == lax.rem(col, GROUP)
    is_real_row = lax.rem(row, parts) == 0
    is_real_col = col < 4 * GROUP
    feed = lax.rem(lax.div(lax.broadcasted_iota(jnp.int32, (inputs, columns), 1), GROUP), 4)
    station = jnp.where(feed < 2, scalars[1], scalars[2])
    pick = (
        lax.broadcasted_iota(jnp.int32, (inputs, columns), 0) == 2 * station + lax.rem(feed, 2)
    ).astype(F32).astype(BF16)
    first_feed = lax.rem(lax.broadcasted_iota(jnp.int32, (GROUP, inputs), 1), 2) == 0
    pair_sum = (
        lax.div(lax.broadcasted_iota(jnp.int32, (inputs, inputs // 2), 0), 2)
        == lax.broadcasted_iota(jnp.int32, (inputs, inputs // 2), 1)
    ).astype(F32).astype(BF16)

    def body(step, carry):
        start = pl.multiple_of(step * GROUP, GROUP)
        here = pl.ds(start, GROUP)
        x = x_ref[:, here, :, :].reshape(depth, inputs)
        picked = jnp.dot(x, pick, preferred_element_type=F32)
        swapped = jnp.where(
            is_real_row, pltpu.roll(picked, depth - 1, 0), -pltpu.roll(picked, 1, 0)
        )
        left = jnp.where(same_channel, jnp.where(is_real_col, picked, swapped), 0.0).astype(BF16)
        out = lax.dot_general(
            left, x, (((0,), (0,)), ((), ())), preferred_element_type=F32
        )

        def rows(part, window, feed_a):
            first = (part * 4 + 2 * window + feed_a) * GROUP
            return out[first : first + GROUP]

        for window in range(2):
            for part in range(2):
                vis_ref[2 * window + part, here, :] = rows(part, window, 0).astype(BF16)
        for part in range(2):
            vis_ref[4 + part, here, :] = jnp.where(
                first_feed, pltpu.roll(rows(part, 1, 1), inputs - 1, 1), rows(part, 0, 1)
            ).astype(BF16)
        pols = []
        for window in range(2):
            x_real, x_imag = rows(0, window, 0), rows(1, window, 0)
            y_real, y_imag = rows(0, window, 1), rows(1, window, 1)
            pols.append(jnp.where(first_feed, x_real - y_imag, -(y_real + x_imag)))
            pols.append(jnp.where(first_feed, x_imag + y_real, x_real - y_imag))
        pol = jnp.concatenate([(0.5 * value).astype(BF16) for value in pols], 0)
        summed = jnp.dot(pol, pair_sum, preferred_element_type=F32).astype(BF16)
        for index in range(4):
            pol_ref[index, here, :] = summed[index * GROUP : (index + 1) * GROUP]
        return carry

    lax.fori_loop(0, x_ref.shape[1] // GROUP, body, 0, unroll=2)


def correlate(voltages, window_stations, first, count):
    times, _, parts, inputs = voltages.shape
    block = math.gcd(count, 64)
    scalars = jnp.concatenate(
        [jnp.reshape(lax.div(first, block), (1,)), window_stations]
    ).astype(jnp.int32)
    return pl.pallas_call(
        correlate_kernel,
        grid_spec=pltpu.PrefetchScalarGridSpec(
            num_scalar_prefetch=1,
            grid=(count // block,),
            in_specs=[pl.BlockSpec((times, block, parts, inputs), lambda i, s: (0, s[0] + i, 0, 0))],
            out_specs=[
                pl.BlockSpec((6, block, inputs), lambda i, s: (0, i, 0)),
                pl.BlockSpec((4, block, inputs // 2), lambda i, s: (0, i, 0)),
            ],
        ),
        out_shape=[
            jax.ShapeDtypeStruct((6, count, inputs), BF16),
            jax.ShapeDtypeStruct((4, count, inputs // 2), BF16),
        ],
        compiler_params=pltpu.CompilerParams(vmem_limit_bytes=40 << 20),
        cost_estimate=pl.CostEstimate(
            flops=count * 16 * 2 * 512 * 256, bytes_accessed=count * 16 * 1024 * 2, transcendentals=0
        ),
        name="correlate",
    )(scalars, voltages)


def transform_kernel(pol_ref, fine_ref, coarse_ref, out_ref, table):
    @pl.when(pl.program_id(0) == 0)
    def _():
        out_ref[...] = jnp.zeros_like(out_ref)

    fine_cos, fine_sin = fine_ref[0], fine_ref[1]
    blocks = DEPTH // LANES
    for block in range(blocks):
        cos = coarse_ref[:, block : block + 1]
        sin = coarse_ref[:, blocks + block : blocks + block + 1]
        table[:, block * LANES : (block + 1) * LANES] = (cos * fine_cos - sin * fine_sin).astype(BF16)
        table[:, DEPTH + block * LANES : DEPTH + (block + 1) * LANES] = (
            sin * fine_cos + cos * fine_sin
        ).astype(BF16)

    def dot(left, right):
        return lax.dot_general(left, right, (((0,), (0,)), ((), ())), preferred_element_type=F32)

    width = 256
    for first in range(0, DEPTH, width):
        cosine = table[:, first : first + width]
        sine = table[:, DEPTH + first : DEPTH + first + width]
        for window in range(2):
            real, imag = pol_ref[2 * window], pol_ref[2 * window + 1]
            out_ref[:, window, 0, first : first + width] += dot(real, cosine) + dot(imag, sine)
            out_ref[:, window, 1, first : first + width] += dot(imag, cosine) - dot(real, sine)


def transform(pol, fine, coarse):
    _, count, stations = pol.shape
    block = math.gcd(count, 256)
    out = pl.pallas_call(
        lambda p, f, c, o, t: transform_kernel(
            p, f, c, o, t
        ),
        grid=(count // block,),
        in_specs=[
            pl.BlockSpec((4, block, stations), lambda i: (0, i, 0)),
            pl.BlockSpec((2, block, LANES), lambda i: (0, i, 0)),
            pl.BlockSpec((block, coarse.shape[1]), lambda i: (i, 0)),
        ],
        out_specs=pl.BlockSpec((stations, 2, 2, DEPTH), lambda i: (0, 0, 0, 0)),
        out_shape=jax.ShapeDtypeStruct((stations, 2, 2, DEPTH), F32),
        scratch_shapes=[pltpu.VMEM((block, 2 * DEPTH), BF16)],
        compiler_params=pltpu.CompilerParams(vmem_limit_bytes=40 << 20),
        cost_estimate=pl.CostEstimate(
            flops=2 * count * 4 * stations * 2 * DEPTH, bytes_accessed=16 << 20, transcendentals=0
        ),
        name="transform",
    )(pol, fine, coarse)
    return out


def tables(channels, flag_weights):
    frequency = 1.0 + (channels.astype(F32) + 0.5) / CHANNELS
    scaled = 2.0 * (1.0 / (frequency * frequency) - 0.5)
    fine_depth = 2.0 * jnp.arange(LANES, dtype=jnp.int32).astype(F32)
    fine_angle = scaled[:, None] * fine_depth[None, :]
    fine = jnp.stack([jnp.cos(fine_angle), jnp.sin(fine_angle)], 0)
    coarse_depth = 2.0 * (jnp.arange(DEPTH // LANES, dtype=jnp.int32) * LANES - DEPTH // 2).astype(F32)
    coarse_angle = coarse_depth[:, None] * scaled[None, :]
    coarse = jnp.concatenate([jnp.cos(coarse_angle), jnp.sin(coarse_angle)], 0) * flag_weights[None, :]
    return fine, coarse.T


def statistics_kernel(vis_ref, flag_ref, out_ref):
    inputs = vis_ref.shape[2]

    def body(step, total):
        here = pl.ds(pl.multiple_of(step * GROUP, GROUP), GROUP)
        flag = flag_ref[here, :]
        values = [vis_ref[index, here, :].astype(F32) for index in range(6)]
        found = []
        for window in range(2):
            xx = values[2 * window : 2 * window + 2]
            xy = [pltpu.roll(value, inputs - 1, 1) for value in xx]
            yy = values[4:6]
            if window == 0:
                yy = [pltpu.roll(value, inputs - 1, 1) for value in yy]
            for left, right in ((xy, yy), (xx, yy), (xy, xx)):
                found.append(left[0] * right[0] + left[1] * right[1])
                found.append(left[1] * right[0] - left[0] * right[1])
            found.append(yy[0] * yy[0] + yy[1] * yy[1])
            found.append(xx[0] * xx[0] + xx[1] * xx[1])
        rows = [jnp.sum(flag * value, 0, keepdims=True) for value in found]
        return total + jnp.concatenate(rows, 0)

    out_ref[...] = lax.fori_loop(
        0, vis_ref.shape[1] // GROUP, body, jnp.zeros(out_ref.shape, F32)
    )


def statistics(vis, flags):
    return pl.pallas_call(
        statistics_kernel,
        out_shape=jax.ShapeDtypeStruct((16, vis.shape[2]), F32),
        compiler_params=pltpu.CompilerParams(vmem_limit_bytes=40 << 20),
        name="statistics",
    )(vis, flags)


def fit_kernel(stations_ref, stats_ref, out_ref):
    count = stats_ref.shape[1]
    lane = lax.broadcasted_iota(jnp.int32, (1, count), 1)
    chosen = [(lane == stations_ref[window]).astype(F32) for window in range(2)]

    def total(value):
        return jnp.sum(value, 1, keepdims=True)

    def field(window, index):
        return stats_ref[8 * window + index : 8 * window + index + 1, :]

    weights = jnp.zeros((1, count), F32)
    for window in range(2):
        weights += chosen[window] * total(field(window, 6)) + field(window, 7)
    weights += 1e-6
    real = jnp.zeros((1, count), F32)
    imag = jnp.zeros((1, count), F32)
    for _ in range(ITERATIONS):
        numer_real = jnp.zeros((1, count), F32)
        numer_imag = jnp.zeros((1, count), F32)
        for window in range(2):
            cross_r, cross_i, mixed_r, mixed_i, side_r, side_i = [
                field(window, index) for index in range(6)
            ]
            near_real = total(chosen[window] * real)
            near_imag = total(chosen[window] * imag)
            row_real = cross_r - (real * mixed_r + imag * mixed_i)
            row_imag = cross_i - (real * mixed_i - imag * mixed_r)
            col_real = side_r - (near_real * mixed_r + near_imag * mixed_i)
            col_imag = -(side_i - (near_imag * mixed_r - near_real * mixed_i))
            numer_real += chosen[window] * total(row_real) + col_real
            numer_imag += chosen[window] * total(row_imag) + col_imag
        real = numer_real / weights
        imag = numer_imag / weights
    out_ref[0:1, :] = real
    out_ref[1:2, :] = imag


def fit(stats, window_stations):
    return pl.pallas_call(
        fit_kernel,
        in_specs=[
            pl.BlockSpec(memory_space=pltpu.SMEM),
            pl.BlockSpec(memory_space=pltpu.VMEM),
        ],
        out_shape=jax.ShapeDtypeStruct((2, stats.shape[1]), F32),
        name="fit",
    )(window_stations, stats)


def add(left, right):
    return (left.astype(F32) + right.astype(F32)).astype(BF16)


def ring_sum(block_of, place, size, axis, pairs):
    running = block_of(lax.rem(place + size - 1, size))
    for step in range(1, size):
        running = lax.ppermute(running, axis, pairs)
        running = add(running, block_of(lax.rem(place + 2 * size - 1 - step, size)))
    return running


def per_device(voltages, window_stations, channel_flags):
    tm_size = lax.axis_size("tm")
    chan_size = lax.axis_size("chan")
    times, local, _, inputs = voltages.shape
    stations = inputs // 2
    tm, chan = lax.axis_index("tm"), lax.axis_index("chan")
    num_z, num_y = NUM_Z, tm_size // NUM_Z
    place_z, place_y = lax.div(tm, num_y), lax.rem(tm, num_y)
    num_x, place_x, core = chan_size // CORES, lax.div(chan, CORES), lax.rem(chan, CORES)
    y_pairs = [
        (z * num_y + y, z * num_y + (y + 1) % num_y) for z in range(num_z) for y in range(num_y)
    ]
    z_pairs = [
        (z * num_y + y, ((z + 1) % num_z) * num_y + y) for z in range(num_z) for y in range(num_y)
    ]
    x_pairs = [(x * CORES + c, ((x + 1) % num_x) * CORES + c) for x in range(num_x) for c in range(CORES)]
    core_pairs = [(x * CORES + c, x * CORES + (c + 1) % CORES) for x in range(num_x) for c in range(CORES)]

    per_y = local // num_y
    per_chunk = per_y // CHUNKS
    per_z = per_chunk // num_z
    order = [lax.rem(place_y + 2 * num_y - 1 - step, num_y) for step in range(num_y)]
    vis, pols, visited = {}, [], []
    for step, y_block in enumerate(order):
        for chunk in range(CHUNKS):
            first = y_block * per_y + chunk * per_chunk
            vis[step, chunk], pol = correlate(voltages, window_stations, first, per_chunk)
            pols.append(pol)
            visited.append(chan * local + first + jnp.arange(per_chunk, dtype=jnp.int32))
    weights = channel_flags.astype(F32)

    finished = []
    for chunk in range(CHUNKS):
        running = vis[0, chunk]
        for step in range(1, num_y):
            running = add(lax.ppermute(running, "tm", y_pairs), vis[step, chunk])
        parts = running.reshape(6, num_z, per_z, inputs)

        def z_block(index, parts=parts):
            return lax.dynamic_index_in_dim(parts, index, 1, keepdims=False)

        finished.append(ring_sum(z_block, place_z, num_z, "tm", z_pairs))
    own_vis = jnp.concatenate(finished, 1)
    own_flags = lax.dynamic_slice(
        weights.reshape(chan_size, num_y, CHUNKS, num_z, per_z),
        (chan, place_y, 0, place_z, 0),
        (1, 1, CHUNKS, 1, per_z),
    ).reshape(-1, 1)

    by_y = lax.dynamic_slice_in_dim(weights, chan * local, local, 0).reshape(num_y, per_y)
    local_flags = jnp.concatenate(
        [lax.dynamic_index_in_dim(by_y, y_block, 0, keepdims=False) for y_block in order]
    )
    fine, coarse = tables(jnp.concatenate(visited), local_flags)
    spectrum = transform(jnp.concatenate(pols, 1), fine, coarse)
    own = stations // (tm_size * chan_size)
    cube = spectrum.astype(BF16).reshape(num_z, num_y, num_x, CORES, own, 2, 2, DEPTH)
    for axis, pairs, place, size, dim in (
        ("chan", core_pairs, core, CORES, 3),
        ("chan", x_pairs, place_x, num_x, 2),
        ("tm", y_pairs, place_y, num_y, 1),
        ("tm", z_pairs, place_z, num_z, 0),
    ):
        def block_of(index, cube=cube, dim=dim):
            return lax.dynamic_index_in_dim(cube, index, dim, keepdims=False)

        cube = ring_sum(block_of, place, size, axis, pairs)
    norm_factor = 1.0 / math.sqrt(CHANNELS * times * tm_size)
    rm_spectrum = (cube.astype(F32) * norm_factor).reshape(1, own, 2, 2, DEPTH)

    stats = statistics(own_vis, own_flags).reshape(16, stations, 2)[:, :, 0]
    stats = lax.psum(stats, ("chan", "tm")) / CHANNELS
    return (rm_spectrum, fit(stats, window_stations))


def solution(mesh):
    return jax.shard_map(
        per_device,
        mesh=mesh,
        in_specs=(P("tm", "chan", None, None), P(), P()),
        out_specs=(P("tm", "chan", None, None, None), P()),
        check_vma=False,
    )
```

```python
import math

import jax
import jax.numpy as jnp
from jax import lax
from jax.experimental import pallas as pl
from jax.experimental.pallas import tpu as pltpu
from jax.sharding import PartitionSpec as P

CHANNELS = 8192
DEPTH = 1024
ITERATIONS = 3
GROUP = 16
LANES = 128
NUM_Z = 4
CORES = 2
CHUNKS = 4
F32 = jnp.float32
BF16 = jnp.bfloat16


def selectors(window_stations, times, parts, inputs):
    depth, columns = times * GROUP * parts, 8 * GROUP
    row = jnp.arange(depth, dtype=jnp.int32)[:, None]
    col = jnp.arange(columns, dtype=jnp.int32)[None, :]
    same = (row // parts) % GROUP == col % GROUP
    real_row, real_col = row % parts == 0, col < 4 * GROUP
    masks = jnp.stack(
        [
            (same & real_col).astype(F32),
            (same & ~real_col & real_row).astype(F32),
            -(same & ~real_col & ~real_row).astype(F32),
        ],
        0,
    )
    feeds = (2 * window_stations[:, None] + jnp.arange(2, dtype=jnp.int32)[None, :]).reshape(-1)
    lane = jnp.arange(inputs, dtype=jnp.int32)[:, None]
    pick = (lane == jnp.tile(jnp.repeat(feeds, GROUP), 2)[None, :]).astype(BF16)
    pair_sum = (lane // 2 == jnp.arange(inputs // 2, dtype=jnp.int32)[None, :]).astype(BF16)
    return masks, pick, pair_sum


def correlate_kernel(scalars, x_ref, mask_ref, pick_ref, pair_ref, vis_ref, pol_ref):
    times, _, parts, inputs = x_ref.shape
    depth = times * GROUP * parts
    first_feed = (lax.broadcasted_iota(jnp.int32, (GROUP, inputs), 1) & 1) == 0

    def body(step, carry):
        start = pl.multiple_of(step * GROUP, GROUP)
        here = pl.ds(start, GROUP)
        x = x_ref[:, here, :, :].reshape(depth, inputs)
        picked = jnp.dot(x, pick_ref[...], preferred_element_type=F32)
        left = (
            picked * mask_ref[0]
            + pltpu.roll(picked, depth - 1, 0) * mask_ref[1]
            + pltpu.roll(picked, 1, 0) * mask_ref[2]
        ).astype(BF16)
        out = lax.dot_general(
            left, x, (((0,), (0,)), ((), ())), preferred_element_type=F32
        )

        def rows(part, window, feed_a):
            first = (part * 4 + 2 * window + feed_a) * GROUP
            return out[first : first + GROUP]

        for window in range(2):
            for part in range(2):
                vis_ref[2 * window + part, here, :] = rows(part, window, 0).astype(BF16)
        for part in range(2):
            vis_ref[4 + part, here, :] = jnp.where(
                first_feed, pltpu.roll(rows(part, 1, 1), inputs - 1, 1), rows(part, 0, 1)
            ).astype(BF16)
        pols = []
        for window in range(2):
            x_real, x_imag = rows(0, window, 0), rows(1, window, 0)
            y_real, y_imag = rows(0, window, 1), rows(1, window, 1)
            pols.append(jnp.where(first_feed, x_real - y_imag, -(y_real + x_imag)))
            pols.append(jnp.where(first_feed, x_imag + y_real, x_real - y_imag))
        pol = jnp.concatenate([(0.5 * value).astype(BF16) for value in pols], 0)
        summed = jnp.dot(pol, pair_ref[...], preferred_element_type=F32).astype(BF16)
        for index in range(4):
            pol_ref[index, here, :] = summed[index * GROUP : (index + 1) * GROUP]
        return carry

    lax.fori_loop(0, x_ref.shape[1] // GROUP, body, 0, unroll=2)


def correlate(voltages, chosen, first, count):
    times, _, parts, inputs = voltages.shape
    block = math.gcd(count, 64)
    scalars = jnp.reshape(lax.div(first, block), (1,)).astype(jnp.int32)
    return pl.pallas_call(
        correlate_kernel,
        grid_spec=pltpu.PrefetchScalarGridSpec(
            num_scalar_prefetch=1,
            grid=(count // block,),
            in_specs=[
                pl.BlockSpec((times, block, parts, inputs), lambda i, s: (0, s[0] + i, 0, 0)),
                pl.BlockSpec(chosen[0].shape, lambda i, s: (0, 0, 0)),
                pl.BlockSpec(chosen[1].shape, lambda i, s: (0, 0)),
                pl.BlockSpec(chosen[2].shape, lambda i, s: (0, 0)),
            ],
            out_specs=[
                pl.BlockSpec((6, block, inputs), lambda i, s: (0, i, 0)),
                pl.BlockSpec((4, block, inputs // 2), lambda i, s: (0, i, 0)),
            ],
        ),
        out_shape=[
            jax.ShapeDtypeStruct((6, count, inputs), BF16),
            jax.ShapeDtypeStruct((4, count, inputs // 2), BF16),
        ],
        compiler_params=pltpu.CompilerParams(vmem_limit_bytes=40 << 20),
        cost_estimate=pl.CostEstimate(
            flops=count * 16 * 2 * 512 * 256, bytes_accessed=count * 16 * 1024 * 2, transcendentals=0
        ),
        name="correlate",
    )(scalars, voltages, *chosen)


def transform_kernel(pol_ref, fine_ref, coarse_ref, out_ref, table, total):
    @pl.when(pl.program_id(0) == 0)
    def _():
        total[...] = jnp.zeros_like(total)

    fine_cos, fine_sin = fine_ref[0], fine_ref[1]
    blocks = DEPTH // LANES
    for block in range(blocks):
        cos = coarse_ref[:, block : block + 1]
        sin = coarse_ref[:, blocks + block : blocks + block + 1]
        table[:, block * LANES : (block + 1) * LANES] = (cos * fine_cos - sin * fine_sin).astype(BF16)
        table[:, DEPTH + block * LANES : DEPTH + (block + 1) * LANES] = (
            sin * fine_cos + cos * fine_sin
        ).astype(BF16)

    def dot(left, right):
        return lax.dot_general(left, right, (((0,), (0,)), ((), ())), preferred_element_type=F32)

    width = 256
    for first in range(0, DEPTH, width):
        cosine = table[:, first : first + width]
        sine = table[:, DEPTH + first : DEPTH + first + width]
        for window in range(2):
            real, imag = pol_ref[2 * window], pol_ref[2 * window + 1]
            total[2 * window, :, first : first + width] += dot(real, cosine) + dot(imag, sine)
            total[2 * window + 1, :, first : first + width] += dot(imag, cosine) - dot(real, sine)

    @pl.when(pl.program_id(0) == pl.num_programs(0) - 1)
    def _():
        out_ref[...] = total[...].astype(BF16)


def transform(pol, fine, coarse):
    _, count, stations = pol.shape
    block = math.gcd(count, 256)
    out = pl.pallas_call(
        transform_kernel,
        grid=(count // block,),
        in_specs=[
            pl.BlockSpec((4, block, stations), lambda i: (0, i, 0)),
            pl.BlockSpec((2, block, LANES), lambda i: (0, i, 0)),
            pl.BlockSpec((block, coarse.shape[1]), lambda i: (i, 0)),
        ],
        out_specs=pl.BlockSpec((4, stations, DEPTH), lambda i: (0, 0, 0)),
        out_shape=jax.ShapeDtypeStruct((4, stations, DEPTH), BF16),
        scratch_shapes=[pltpu.VMEM((block, 2 * DEPTH), BF16), pltpu.VMEM((4, stations, DEPTH), F32)],
        compiler_params=pltpu.CompilerParams(vmem_limit_bytes=40 << 20),
        cost_estimate=pl.CostEstimate(
            flops=2 * count * 4 * stations * 2 * DEPTH, bytes_accessed=16 << 20, transcendentals=0
        ),
        name="transform",
    )(pol, fine, coarse)
    return out


def tables(channels, flag_weights):
    frequency = 1.0 + (channels.astype(F32) + 0.5) / CHANNELS
    scaled = 2.0 * (1.0 / (frequency * frequency) - 0.5)
    fine_depth = 2.0 * jnp.arange(LANES, dtype=jnp.int32).astype(F32)
    fine_angle = scaled[:, None] * fine_depth[None, :]
    fine = jnp.stack([jnp.cos(fine_angle), jnp.sin(fine_angle)], 0)
    coarse_depth = 2.0 * (jnp.arange(DEPTH // LANES, dtype=jnp.int32) * LANES - DEPTH // 2).astype(F32)
    coarse_angle = coarse_depth[:, None] * scaled[None, :]
    coarse = jnp.concatenate([jnp.cos(coarse_angle), jnp.sin(coarse_angle)], 0) * flag_weights[None, :]
    return fine, coarse.T


def statistics_kernel(vis_ref, flag_ref, out_ref):
    inputs = vis_ref.shape[2]

    def body(step, total):
        here = pl.ds(pl.multiple_of(step * GROUP, GROUP), GROUP)
        flag = flag_ref[here, :]
        values = [vis_ref[index, here, :].astype(F32) for index in range(6)]
        found = []
        for window in range(2):
            xx = values[2 * window : 2 * window + 2]
            xy = [pltpu.roll(value, inputs - 1, 1) for value in xx]
            yy = values[4:6]
            if window == 0:
                yy = [pltpu.roll(value, inputs - 1, 1) for value in yy]
            for left, right in ((xy, yy), (xx, yy), (xy, xx)):
                found.append(left[0] * right[0] + left[1] * right[1])
                found.append(left[1] * right[0] - left[0] * right[1])
            found.append(yy[0] * yy[0] + yy[1] * yy[1])
            found.append(xx[0] * xx[0] + xx[1] * xx[1])
        rows = [jnp.sum(flag * value, 0, keepdims=True) for value in found]
        return total + jnp.concatenate(rows, 0)

    out_ref[...] = lax.fori_loop(
        0, vis_ref.shape[1] // GROUP, body, jnp.zeros(out_ref.shape, F32)
    )


def statistics(vis, flags):
    return pl.pallas_call(
        statistics_kernel,
        out_shape=jax.ShapeDtypeStruct((16, vis.shape[2]), F32),
        compiler_params=pltpu.CompilerParams(vmem_limit_bytes=40 << 20),
        name="statistics",
    )(vis, flags)


def fit_kernel(stations_ref, stats_ref, out_ref):
    count = stats_ref.shape[1]
    lane = lax.broadcasted_iota(jnp.int32, (1, count), 1)
    chosen = [(lane == stations_ref[window]).astype(F32) for window in range(2)]

    def total(value):
        return jnp.sum(value, 1, keepdims=True)

    def field(window, index):
        return stats_ref[8 * window + index : 8 * window + index + 1, :]

    weights = jnp.zeros((1, count), F32)
    for window in range(2):
        weights += chosen[window] * total(field(window, 6)) + field(window, 7)
    weights += 1e-6
    real = jnp.zeros((1, count), F32)
    imag = jnp.zeros((1, count), F32)
    for _ in range(ITERATIONS):
        numer_real = jnp.zeros((1, count), F32)
        numer_imag = jnp.zeros((1, count), F32)
        for window in range(2):
            cross_r, cross_i, mixed_r, mixed_i, side_r, side_i = [
                field(window, index) for index in range(6)
            ]
            near_real = total(chosen[window] * real)
            near_imag = total(chosen[window] * imag)
            row_real = cross_r - (real * mixed_r + imag * mixed_i)
            row_imag = cross_i - (real * mixed_i - imag * mixed_r)
            col_real = side_r - (near_real * mixed_r + near_imag * mixed_i)
            col_imag = -(side_i - (near_imag * mixed_r - near_real * mixed_i))
            numer_real += chosen[window] * total(row_real) + col_real
            numer_imag += chosen[window] * total(row_imag) + col_imag
        real = numer_real / weights
        imag = numer_imag / weights
    out_ref[0:1, :] = real
    out_ref[1:2, :] = imag


def fit(stats, window_stations):
    return pl.pallas_call(
        fit_kernel,
        in_specs=[
            pl.BlockSpec(memory_space=pltpu.SMEM),
            pl.BlockSpec(memory_space=pltpu.VMEM),
        ],
        out_shape=jax.ShapeDtypeStruct((2, stats.shape[1]), F32),
        name="fit",
    )(window_stations, stats)


def add(left, right):
    return (left.astype(F32) + right.astype(F32)).astype(BF16)


def ring_sum(block_of, place, size, axis, pairs):
    running = block_of(lax.rem(place + size - 1, size))
    for step in range(1, size):
        running = lax.ppermute(running, axis, pairs)
        running = add(running, block_of(lax.rem(place + 2 * size - 1 - step, size)))
    return running


def after(value, *others):
    return lax.optimization_barrier((value, *others))[0]


def exchange_sum(value, axis, size):
    terms = [value]
    for flip in range(1, size):
        terms.append(lax.ppermute(value, axis, [(place, place ^ flip) for place in range(size)]))
    while len(terms) > 1:
        terms = [terms[index] + terms[index + 1] for index in range(0, len(terms), 2)]
    return terms[0]


def per_device(voltages, window_stations, channel_flags):
    tm_size = lax.axis_size("tm")
    chan_size = lax.axis_size("chan")
    times, local, _, inputs = voltages.shape
    stations = inputs // 2
    tm, chan = lax.axis_index("tm"), lax.axis_index("chan")
    num_z, num_y = NUM_Z, tm_size // NUM_Z
    place_z, place_y = lax.div(tm, num_y), lax.rem(tm, num_y)
    num_x, place_x, core = chan_size // CORES, lax.div(chan, CORES), lax.rem(chan, CORES)
    y_pairs = [
        (z * num_y + y, z * num_y + (y + 1) % num_y) for z in range(num_z) for y in range(num_y)
    ]
    z_pairs = [
        (z * num_y + y, ((z + 1) % num_z) * num_y + y) for z in range(num_z) for y in range(num_y)
    ]
    x_pairs = [(x * CORES + c, ((x + 1) % num_x) * CORES + c) for x in range(num_x) for c in range(CORES)]
    core_pairs = [(x * CORES + c, x * CORES + (c + 1) % CORES) for x in range(num_x) for c in range(CORES)]

    per_y = local // num_y
    per_chunk = per_y // CHUNKS
    per_z = per_chunk // num_z
    order = [lax.rem(place_y + 2 * num_y - 1 - step, num_y) for step in range(num_y)]
    chosen = selectors(window_stations, times, voltages.shape[2], inputs)
    pols, arrived = [], []
    for chunk in range(CHUNKS):
        part, pol = correlate(voltages, chosen, order[0] * per_y + chunk * per_chunk, per_chunk)
        pols.append(pol)
        arrived.append(lax.ppermute(part, "tm", y_pairs))
    own = []
    for y_block in order[1:]:
        first = after(y_block * per_y, arrived[0], pols[CHUNKS - 1])
        part, pol = correlate(voltages, chosen, first, per_y)
        own.append(part)
        pols.append(pol)
    weights = channel_flags.astype(F32)
    by_y = lax.dynamic_slice_in_dim(weights, chan * local, local, 0).reshape(num_y, per_y)
    local_flags = jnp.concatenate(
        [lax.dynamic_index_in_dim(by_y, y_block, 0, keepdims=False) for y_block in order]
    )
    local_channels = chan * local + jnp.arange(per_y, dtype=jnp.int32)
    visited = jnp.concatenate([local_channels + y_block * per_y for y_block in order])
    fine, coarse = tables(visited, local_flags)
    spectrum = transform(jnp.concatenate(pols, 1), fine, coarse)

    finished = []
    for chunk in range(CHUNKS):
        running = arrived[chunk]
        if finished:
            running = after(running, finished[-1], spectrum)
        for step, part in enumerate(own):
            if step:
                running = lax.ppermute(running, "tm", y_pairs)
            running = add(running, part[:, chunk * per_chunk : (chunk + 1) * per_chunk])
        parts = running.reshape(6, num_z, per_z, inputs)

        def z_block(index, parts=parts):
            return lax.dynamic_index_in_dim(parts, index, 1, keepdims=False)

        finished.append(ring_sum(z_block, place_z, num_z, "tm", z_pairs))
    own_vis = jnp.concatenate(finished, 1)
    own_flags = lax.dynamic_slice(
        weights.reshape(chan_size, num_y, CHUNKS, num_z, per_z),
        (chan, place_y, 0, place_z, 0),
        (1, 1, CHUNKS, 1, per_z),
    ).reshape(-1, 1)

    kept = stations // (tm_size * chan_size)
    cube = spectrum.reshape(4, num_z, num_y, num_x, CORES, kept, DEPTH)
    for axis, pairs, place, size, dim in (
        ("chan", core_pairs, core, CORES, 4),
        ("chan", x_pairs, place_x, num_x, 3),
        ("tm", y_pairs, place_y, num_y, 2),
        ("tm", z_pairs, place_z, num_z, 1),
    ):
        def block_of(index, cube=cube, dim=dim):
            return lax.dynamic_index_in_dim(cube, index, dim, keepdims=False)

        cube = ring_sum(block_of, place, size, axis, pairs)
    norm_factor = 1.0 / math.sqrt(CHANNELS * times * tm_size)
    rm_spectrum = jnp.swapaxes(cube.astype(F32) * norm_factor, 0, 1)
    rm_spectrum = rm_spectrum.reshape(1, kept, 2, 2, DEPTH)

    stats = statistics(own_vis, own_flags).reshape(16, stations, 2)[:, :, 0]
    stats = exchange_sum(exchange_sum(stats, "chan", chan_size), "tm", tm_size) / CHANNELS
    return (rm_spectrum, fit(stats, window_stations))


def solution(mesh):
    return jax.shard_map(
        per_device,
        mesh=mesh,
        in_specs=(P("tm", "chan", None, None), P(), P()),
        out_specs=(P("tm", "chan", None, None, None), P()),
        check_vma=False,
    )
```

```python
import math

import jax
import jax.numpy as jnp
from jax import lax
from jax.experimental import pallas as pl
from jax.experimental.pallas import tpu as pltpu
from jax.sharding import PartitionSpec as P

CHANNELS = 8192
DEPTH = 1024
ITERATIONS = 3
GROUP = 16
LANES = 128
NUM_Z = 4
CORES = 2
CHUNKS = (3, 3, 2)
F32 = jnp.float32
BF16 = jnp.bfloat16


def selectors(window_stations, times, parts, inputs):
    depth, columns = times * GROUP * parts, 8 * GROUP
    row = jnp.arange(depth, dtype=jnp.int32)[:, None]
    col = jnp.arange(columns, dtype=jnp.int32)[None, :]
    same = (row // parts) % GROUP == col % GROUP
    real_row, real_col = row % parts == 0, col < 4 * GROUP
    masks = jnp.stack(
        [
            (same & real_col).astype(F32),
            (same & ~real_col & real_row).astype(F32),
            -(same & ~real_col & ~real_row).astype(F32),
        ],
        0,
    )
    feeds = (2 * window_stations[:, None] + jnp.arange(2, dtype=jnp.int32)[None, :]).reshape(-1)
    lane = jnp.arange(inputs, dtype=jnp.int32)[:, None]
    pick = (lane == jnp.tile(jnp.repeat(feeds, GROUP), 2)[None, :]).astype(BF16)
    pair_sum = (lane // 2 == jnp.arange(inputs // 2, dtype=jnp.int32)[None, :]).astype(BF16)
    return masks, pick, pair_sum


def correlate_kernel(scalars, x_ref, mask_ref, pick_ref, pair_ref, vis_ref, pol_ref):
    times, _, parts, inputs = x_ref.shape
    depth = times * GROUP * parts
    first_feed = (lax.broadcasted_iota(jnp.int32, (GROUP, inputs), 1) & 1) == 0

    def body(step, carry):
        start = pl.multiple_of(step * GROUP, GROUP)
        here = pl.ds(start, GROUP)
        x = x_ref[:, here, :, :].reshape(depth, inputs)
        picked = jnp.dot(x, pick_ref[...], preferred_element_type=F32)
        left = (
            picked * mask_ref[0]
            + pltpu.roll(picked, depth - 1, 0) * mask_ref[1]
            + pltpu.roll(picked, 1, 0) * mask_ref[2]
        ).astype(BF16)
        out = lax.dot_general(
            left, x, (((0,), (0,)), ((), ())), preferred_element_type=F32
        )

        def rows(part, window, feed_a):
            first = (part * 4 + 2 * window + feed_a) * GROUP
            return out[first : first + GROUP]

        for window in range(2):
            for part in range(2):
                vis_ref[2 * window + part, here, :] = rows(part, window, 0).astype(BF16)
        for part in range(2):
            vis_ref[4 + part, here, :] = jnp.where(
                first_feed, pltpu.roll(rows(part, 1, 1), inputs - 1, 1), rows(part, 0, 1)
            ).astype(BF16)
        pols = []
        for window in range(2):
            x_real, x_imag = rows(0, window, 0), rows(1, window, 0)
            y_real, y_imag = rows(0, window, 1), rows(1, window, 1)
            pols.append(jnp.where(first_feed, x_real - y_imag, -(y_real + x_imag)))
            pols.append(jnp.where(first_feed, x_imag + y_real, x_real - y_imag))
        pol = jnp.concatenate([(0.5 * value).astype(BF16) for value in pols], 0)
        summed = jnp.dot(pol, pair_ref[...], preferred_element_type=F32).astype(BF16)
        for index in range(4):
            pol_ref[index, here, :] = summed[index * GROUP : (index + 1) * GROUP]
        return carry

    lax.fori_loop(0, x_ref.shape[1] // GROUP, body, 0, unroll=2)


def correlate(voltages, chosen, first, count):
    times, _, parts, inputs = voltages.shape
    block = math.gcd(count, 64)
    scalars = jnp.reshape(lax.div(first, block), (1,)).astype(jnp.int32)
    return pl.pallas_call(
        correlate_kernel,
        grid_spec=pltpu.PrefetchScalarGridSpec(
            num_scalar_prefetch=1,
            grid=(count // block,),
            in_specs=[
                pl.BlockSpec((times, block, parts, inputs), lambda i, s: (0, s[0] + i, 0, 0)),
                pl.BlockSpec(chosen[0].shape, lambda i, s: (0, 0, 0)),
                pl.BlockSpec(chosen[1].shape, lambda i, s: (0, 0)),
                pl.BlockSpec(chosen[2].shape, lambda i, s: (0, 0)),
            ],
            out_specs=[
                pl.BlockSpec((6, block, inputs), lambda i, s: (0, i, 0)),
                pl.BlockSpec((4, block, inputs // 2), lambda i, s: (0, i, 0)),
            ],
        ),
        out_shape=[
            jax.ShapeDtypeStruct((6, count, inputs), BF16),
            jax.ShapeDtypeStruct((4, count, inputs // 2), BF16),
        ],
        compiler_params=pltpu.CompilerParams(vmem_limit_bytes=40 << 20),
        cost_estimate=pl.CostEstimate(flops=1024, bytes_accessed=1024, transcendentals=0),
        name="correlate",
    )(scalars, voltages, *chosen)


def transform_kernel(pol_ref, fine_ref, coarse_ref, out_ref, table, total):
    @pl.when(pl.program_id(0) == 0)
    def _():
        total[...] = jnp.zeros_like(total)

    fine_cos, fine_sin = fine_ref[0], fine_ref[1]
    blocks = DEPTH // LANES
    for block in range(blocks):
        cos = coarse_ref[:, block : block + 1]
        sin = coarse_ref[:, blocks + block : blocks + block + 1]
        table[:, block * LANES : (block + 1) * LANES] = (cos * fine_cos - sin * fine_sin).astype(BF16)
        table[:, DEPTH + block * LANES : DEPTH + (block + 1) * LANES] = (
            sin * fine_cos + cos * fine_sin
        ).astype(BF16)

    def dot(left, right):
        return lax.dot_general(left, right, (((0,), (0,)), ((), ())), preferred_element_type=F32)

    width = 256
    for first in range(0, DEPTH, width):
        cosine = table[:, first : first + width]
        sine = table[:, DEPTH + first : DEPTH + first + width]
        for window in range(2):
            real, imag = pol_ref[2 * window], pol_ref[2 * window + 1]
            total[2 * window, :, first : first + width] += dot(real, cosine) + dot(imag, sine)
            total[2 * window + 1, :, first : first + width] += dot(imag, cosine) - dot(real, sine)

    @pl.when(pl.program_id(0) == pl.num_programs(0) - 1)
    def _():
        out_ref[...] = total[...].astype(BF16)


def transform(pol, fine, coarse):
    _, count, stations = pol.shape
    block = math.gcd(count, 256)
    out = pl.pallas_call(
        transform_kernel,
        grid=(count // block,),
        in_specs=[
            pl.BlockSpec((4, block, stations), lambda i: (0, i, 0)),
            pl.BlockSpec((2, block, LANES), lambda i: (0, i, 0)),
            pl.BlockSpec((block, coarse.shape[1]), lambda i: (i, 0)),
        ],
        out_specs=pl.BlockSpec((4, stations, DEPTH), lambda i: (0, 0, 0)),
        out_shape=jax.ShapeDtypeStruct((4, stations, DEPTH), BF16),
        scratch_shapes=[pltpu.VMEM((block, 2 * DEPTH), BF16), pltpu.VMEM((4, stations, DEPTH), F32)],
        compiler_params=pltpu.CompilerParams(vmem_limit_bytes=40 << 20),
        cost_estimate=pl.CostEstimate(flops=1024, bytes_accessed=1024, transcendentals=0),
        name="transform",
    )(pol, fine, coarse)
    return out


def tables(channels, flag_weights):
    frequency = 1.0 + (channels.astype(F32) + 0.5) / CHANNELS
    scaled = 2.0 * (1.0 / (frequency * frequency) - 0.5)
    fine_depth = 2.0 * jnp.arange(LANES, dtype=jnp.int32).astype(F32)
    fine_angle = scaled[:, None] * fine_depth[None, :]
    fine = jnp.stack([jnp.cos(fine_angle), jnp.sin(fine_angle)], 0)
    coarse_depth = 2.0 * (jnp.arange(DEPTH // LANES, dtype=jnp.int32) * LANES - DEPTH // 2).astype(F32)
    coarse_angle = coarse_depth[:, None] * scaled[None, :]
    coarse = jnp.concatenate([jnp.cos(coarse_angle), jnp.sin(coarse_angle)], 0) * flag_weights[None, :]
    return fine, coarse.T


def statistics_kernel(vis_ref, flag_ref, out_ref):
    inputs = vis_ref.shape[2]

    def body(step, total):
        here = pl.ds(pl.multiple_of(step * GROUP, GROUP), GROUP)
        flag = flag_ref[here, :]
        values = [vis_ref[index, here, :].astype(F32) for index in range(6)]
        found = []
        for window in range(2):
            xx = values[2 * window : 2 * window + 2]
            xy = [pltpu.roll(value, inputs - 1, 1) for value in xx]
            yy = values[4:6]
            if window == 0:
                yy = [pltpu.roll(value, inputs - 1, 1) for value in yy]
            for left, right in ((xy, yy), (xx, yy), (xy, xx)):
                found.append(left[0] * right[0] + left[1] * right[1])
                found.append(left[1] * right[0] - left[0] * right[1])
            found.append(yy[0] * yy[0] + yy[1] * yy[1])
            found.append(xx[0] * xx[0] + xx[1] * xx[1])
        rows = [jnp.sum(flag * value, 0, keepdims=True) for value in found]
        return total + jnp.concatenate(rows, 0)

    out_ref[...] = lax.fori_loop(
        0, vis_ref.shape[1] // GROUP, body, jnp.zeros(out_ref.shape, F32)
    )


def statistics(vis, flags):
    return pl.pallas_call(
        statistics_kernel,
        out_shape=jax.ShapeDtypeStruct((16, vis.shape[2]), F32),
        compiler_params=pltpu.CompilerParams(vmem_limit_bytes=40 << 20),
        name="statistics",
    )(vis, flags)


def fit_kernel(stations_ref, stats_ref, out_ref):
    count = stats_ref.shape[1]
    lane = lax.broadcasted_iota(jnp.int32, (1, count), 1)
    chosen = [(lane == stations_ref[window]).astype(F32) for window in range(2)]

    def total(value):
        return jnp.sum(value, 1, keepdims=True)

    def field(window, index):
        return stats_ref[8 * window + index : 8 * window + index + 1, :]

    weights = jnp.zeros((1, count), F32)
    for window in range(2):
        weights += chosen[window] * total(field(window, 6)) + field(window, 7)
    weights += 1e-6
    real = jnp.zeros((1, count), F32)
    imag = jnp.zeros((1, count), F32)
    for _ in range(ITERATIONS):
        numer_real = jnp.zeros((1, count), F32)
        numer_imag = jnp.zeros((1, count), F32)
        for window in range(2):
            cross_r, cross_i, mixed_r, mixed_i, side_r, side_i = [
                field(window, index) for index in range(6)
            ]
            near_real = total(chosen[window] * real)
            near_imag = total(chosen[window] * imag)
            row_real = cross_r - (real * mixed_r + imag * mixed_i)
            row_imag = cross_i - (real * mixed_i - imag * mixed_r)
            col_real = side_r - (near_real * mixed_r + near_imag * mixed_i)
            col_imag = -(side_i - (near_imag * mixed_r - near_real * mixed_i))
            numer_real += chosen[window] * total(row_real) + col_real
            numer_imag += chosen[window] * total(row_imag) + col_imag
        real = numer_real / weights
        imag = numer_imag / weights
    out_ref[0:1, :] = real
    out_ref[1:2, :] = imag


def fit(stats, window_stations):
    return pl.pallas_call(
        fit_kernel,
        in_specs=[
            pl.BlockSpec(memory_space=pltpu.SMEM),
            pl.BlockSpec(memory_space=pltpu.VMEM),
        ],
        out_shape=jax.ShapeDtypeStruct((2, stats.shape[1]), F32),
        name="fit",
    )(window_stations, stats)


def add(left, right):
    return (left.astype(F32) + right.astype(F32)).astype(BF16)


def ring_sum(block_of, place, size, axis, pairs, before=()):
    running = block_of(lax.rem(place + size - 1, size))
    for step in range(1, size):
        running = after(lax.ppermute(running, axis, pairs), *before)
        running = add(running, block_of(lax.rem(place + 2 * size - 1 - step, size)))
    return running


def after(value, *others):
    return lax.optimization_barrier((value, *others))[0]


def exchange_sum(value, axis, size, unit, count):
    terms = [value]
    for flip in range(unit, unit * count, unit):
        terms.append(lax.ppermute(value, axis, [(place, place ^ flip) for place in range(size)]))
    while len(terms) > 1:
        terms = [terms[index] + terms[index + 1] for index in range(0, len(terms), 2)]
    return terms[0]


def per_device(voltages, window_stations, channel_flags):
    tm_size = lax.axis_size("tm")
    chan_size = lax.axis_size("chan")
    times, local, _, inputs = voltages.shape
    stations = inputs // 2
    tm, chan = lax.axis_index("tm"), lax.axis_index("chan")
    num_z, num_y = NUM_Z, tm_size // NUM_Z
    place_z, place_y = lax.div(tm, num_y), lax.rem(tm, num_y)
    num_x, place_x, core = chan_size // CORES, lax.div(chan, CORES), lax.rem(chan, CORES)
    y_pairs = [
        (z * num_y + y, z * num_y + (y + 1) % num_y) for z in range(num_z) for y in range(num_y)
    ]
    z_pairs = [
        (z * num_y + y, ((z + 1) % num_z) * num_y + y) for z in range(num_z) for y in range(num_y)
    ]
    x_pairs = [(x * CORES + c, ((x + 1) % num_x) * CORES + c) for x in range(num_x) for c in range(CORES)]
    core_pairs = [(x * CORES + c, x * CORES + (c + 1) % CORES) for x in range(num_x) for c in range(CORES)]

    per_y = local // num_y
    sizes = [share * per_y // sum(CHUNKS) for share in CHUNKS]
    starts = [sum(sizes[:chunk]) for chunk in range(len(sizes))]
    order = [lax.rem(place_y + 2 * num_y - 1 - step, num_y) for step in range(num_y)]
    chosen = selectors(window_stations, times, voltages.shape[2], inputs)
    pols, arrived = [], []
    for start, size in zip(starts, sizes):
        part, pol = correlate(voltages, chosen, order[0] * per_y + start, size)
        pols.append(pol)
        arrived.append(lax.ppermute(part, "tm", y_pairs))
    own = []
    for y_block in order[1:]:
        pieces = []
        for chunk, (start, size) in enumerate(zip(starts, sizes)):
            first = after(y_block * per_y + start, pols[len(sizes) - 1], *arrived[: min(chunk, 1)])
            part, pol = correlate(voltages, chosen, first, size)
            pieces.append(part)
            pols.append(pol)
        own.append(pieces)
    weights = channel_flags.astype(F32)
    by_y = lax.dynamic_slice_in_dim(weights, chan * local, local, 0).reshape(num_y, per_y)
    local_flags = jnp.concatenate(
        [lax.dynamic_index_in_dim(by_y, y_block, 0, keepdims=False) for y_block in order]
    )
    local_channels = chan * local + jnp.arange(per_y, dtype=jnp.int32)
    visited = jnp.concatenate([local_channels + y_block * per_y for y_block in order])
    fine, coarse = tables(visited, local_flags)

    finished = []
    for chunk, size in enumerate(sizes):
        running = arrived[chunk]
        if finished:
            running = after(running, finished[0])
        for step, part in enumerate(own):
            if step:
                running = lax.ppermute(running, "tm", y_pairs)
            running = add(running, part[chunk])
        parts = running.reshape(6, num_z, size // num_z, inputs)

        def z_block(index, parts=parts):
            return lax.dynamic_index_in_dim(parts, index, 1, keepdims=False)

        before = (arrived[2],) if chunk == 1 else ()
        finished.append(ring_sum(z_block, place_z, num_z, "tm", z_pairs, before))
    spectrum = transform(after(jnp.concatenate(pols, 1), arrived[2], finished[0]), fine, coarse)
    own_vis = jnp.concatenate(finished, 1)
    own_first = chan * local + place_y * per_y
    own_flags = jnp.concatenate(
        [
            lax.dynamic_slice_in_dim(
                weights, own_first + start + place_z * (size // num_z), size // num_z
            )
            for start, size in zip(starts, sizes)
        ]
    ).reshape(-1, 1)

    kept = stations // (tm_size * chan_size)
    cube = spectrum.reshape(4, num_z, num_y, num_x, CORES, kept, DEPTH)
    for axis, pairs, place, size, dim in (
        ("chan", core_pairs, core, CORES, 4),
        ("chan", x_pairs, place_x, num_x, 3),
        ("tm", y_pairs, place_y, num_y, 2),
        ("tm", z_pairs, place_z, num_z, 1),
    ):
        def block_of(index, cube=cube, dim=dim):
            return lax.dynamic_index_in_dim(cube, index, dim, keepdims=False)

        cube = ring_sum(block_of, place, size, axis, pairs)
    norm_factor = 1.0 / math.sqrt(CHANNELS * times * tm_size)
    rm_spectrum = jnp.swapaxes(cube.astype(F32) * norm_factor, 0, 1)
    rm_spectrum = rm_spectrum.reshape(1, kept, 2, 2, DEPTH)

    stats = statistics(own_vis, own_flags).reshape(16, stations, 2)[:, :, 0]
    stats = exchange_sum(stats, "chan", chan_size, 1, chan_size)
    stats = exchange_sum(stats, "tm", tm_size, 1, num_y)
    stats = exchange_sum(stats, "tm", tm_size, num_y, num_z) / CHANNELS
    return (rm_spectrum, fit(stats, window_stations))


def solution(mesh):
    return jax.shard_map(
        per_device,
        mesh=mesh,
        in_specs=(P("tm", "chan", None, None), P(), P()),
        out_specs=(P("tm", "chan", None, None, None), P()),
        check_vma=False,
    )
```
